32 devices in a mesh: mesh: 16 (over z, y, x), panel: 2 (over core).
Axes of the slice: x: 2, y: 2, z: 4, core: 2. Of those that a mesh axis runs over, the one named last changes fastest.
Arguments:
- basis_vectors: bfloat16 [128, 128, 192], P('mesh', 'panel'), may hold values from -1 to 1
- stiffness_blocks: bfloat16 [896, 192, 192], P('mesh'), may hold values from -0.21875 to 0.21875
- block_rows: int32 [896], P('mesh'), may hold values from 0 to 7
- block_columns: int32 [896], P('mesh'), may hold values from 0 to 23
- density: float32 [896], P('mesh'), may hold values from 0.1 to 1
- block_counts: int32 [16], P('mesh'), may hold values from 14 to 56, as said below
- send_list: int32 [256], P('mesh'), may hold values from 0 to 7
Outputs:
- reduced: float32 [128, 128], P('panel', 'mesh')
The draws below stay inside these ranges and needn't reach their ends.
Inputs may be any that keep to these rules, and one draw needn't show every extreme that they name: `block_counts`: in every draw some partition holds exactly 56 and another exactly 14.
All inputs are finite; a program needn't handle non-finite values.
Results may differ from the reference program's by a relative error of at most 0.0029.
Values may be sent and summed in bfloat16 or wider, within the bound.
A program may use at most 64 MiB of HBM per device.

```python
import jax
import jax.numpy as jnp
from jax import lax

B = 192
NB_DEV = 8
NEIGH = 4
GMAX = 4
CAP = 56
RANKS = 128
NCLUST = 128
NBLK = 896
N_MESH = 16


def draw_block_counts(key, part):
    first_key = jax.random.fold_in(key, 11)
    second_key = jax.random.fold_in(key, 12)
    third_key = jax.random.fold_in(key, 13)
    drawn = jax.random.randint(first_key, (N_MESH,), CAP // 4, CAP + 1)
    fullest = jax.random.randint(second_key, (), 0, N_MESH)
    lightest = (fullest + 1 + jax.random.randint(third_key, (), 0, N_MESH - 1)) % N_MESH
    positions = jnp.arange(N_MESH)
    counts = jnp.where(positions == fullest, CAP, drawn)
    counts = jnp.where(positions == lightest, CAP // 4, counts)
    return counts.astype(jnp.int32)


def plant(values, key, least, top_value):
    spot = [jax.random.randint(jax.random.fold_in(key, axis), (), 0, length) for axis, length in enumerate(values.shape)]
    widest = values.shape.index(max(values.shape))
    beside = spot[:widest] + [(spot[widest] + 1) % values.shape[widest]] + spot[widest + 1:]
    return values.at[tuple(spot)].set(least).at[tuple(beside)].set(top_value)


def steps_of(stream_key, extent, cuts, smallest, high):
    def one(axis_at, blocks):
        heights = jax.random.uniform(jax.random.fold_in(jax.random.fold_in(stream_key, 6), axis_at), (blocks,), jnp.float32, smallest / len(cuts), high / len(cuts))
        return jnp.repeat(jnp.exp(heights), extent[axis_at] // blocks).reshape((-1,) + (1,) * (len(extent) - axis_at - 1))

    level = one(*cuts[0])
    for cut in cuts[1:]:
        level = level * one(*cut)
    return level


def normal_values(stream_key, dims, spread, limit, pieces=(), held_as=jnp.bfloat16):
    values = jax.random.normal(stream_key, dims, jnp.float32) * spread
    if len(pieces) > 0:
        values = steps_of(stream_key, dims, pieces, -0.22, 0.18) * values
    return jnp.clip(values, min=-limit, max=limit).astype(held_as)


def setup_inputs(seed: int = 0) -> dict:
    splits = jax.random.split(jax.random.key(seed), 8)
    return {
        "basis_vectors": normal_values(splits[0], (NCLUST, RANKS, B), (2.0 * (NCLUST * B) ** -0.25), 1.0, ((0, 16), (1, 2))),
        "stiffness_blocks": normal_values(splits[1], (NBLK, B, B), (4 * B) ** -0.5, 0.21875, ((0, 16),)),
        "block_rows": plant(jax.random.randint(splits[2], (NBLK,), 0, NB_DEV), jax.random.fold_in(splits[2], 1), 0, NB_DEV - 1).astype(jnp.int32),
        "block_columns": plant(jax.random.randint(splits[3], (NBLK,), 0, NB_DEV + NEIGH * GMAX), jax.random.fold_in(splits[3], 1), 0, (NB_DEV + NEIGH * GMAX) - 1).astype(jnp.int32),
        "density": jnp.clip(0.1 + 0.9 * jax.random.uniform(splits[4], (NBLK,), jnp.float32) ** steps_of(splits[4], (NBLK,), ((0, 16),), -0.2, 0.2), 0.1, 1.0),
        "block_counts": draw_block_counts(jax.random.fold_in(splits[7], 71), 0),
        "send_list": plant(jax.random.randint(splits[6], (N_MESH * NEIGH * GMAX,), 0, NB_DEV), jax.random.fold_in(splits[6], 1), 0, NB_DEV - 1).astype(jnp.int32),
    }


neighbour_offsets = (1, -1, 2, -2)


def reference(basis_vectors, stiffness_blocks, block_rows, block_columns, density, block_counts, send_list):
    offsets = jnp.array(neighbour_offsets, jnp.int32)
    sends = send_list.reshape(N_MESH, NEIGH, GMAX)

    def one_part(running, partition):
        first_block = (partition * CAP).astype(jnp.int32)
        part_blocks = lax.dynamic_slice_in_dim(stiffness_blocks, first_block, CAP, 0)
        rows_here = lax.dynamic_slice_in_dim(block_rows, first_block, CAP, 0)
        columns = lax.dynamic_slice_in_dim(block_columns, first_block, CAP, 0)
        density_here = lax.dynamic_slice_in_dim(density, first_block, CAP, 0)
        ghost_slot = jnp.maximum(columns - NB_DEV, 0)
        neighbour = ghost_slot // GMAX
        within = ghost_slot % GMAX
        sender = (partition - offsets[neighbour]) % N_MESH
        ghost_cluster = sender * NB_DEV + sends[sender, neighbour, within]
        source = jnp.where(columns < NB_DEV, partition * NB_DEV + columns, ghost_cluster).astype(jnp.int32)
        sources = basis_vectors[source].astype(jnp.float32)
        product = jnp.einsum("bpj,bij->bpi", sources, part_blocks.astype(jnp.float32), precision=lax.Precision.HIGHEST)
        active = jnp.arange(CAP, dtype=jnp.int32) < block_counts[partition]
        scale = jnp.where(active, 1e-3 + density_here ** 3, jnp.float32(0.0))
        selector = (rows_here[None, :] == jnp.arange(NB_DEV, dtype=jnp.int32)[:, None]).astype(jnp.float32) * scale[None, :]
        products = jnp.einsum("nb,bpi->npi", selector, product, precision=lax.Precision.HIGHEST).astype(jnp.bfloat16)
        own_slabs = lax.dynamic_slice_in_dim(basis_vectors, (partition * NB_DEV).astype(jnp.int32), NB_DEV, 0)
        tile = jnp.einsum("npc,nqc->pq", own_slabs.astype(jnp.float32), products.astype(jnp.float32), precision=lax.Precision.HIGHEST)
        return running + tile, None

    reduced, unused = lax.scan(one_part, jnp.zeros((RANKS, RANKS), jnp.float32), jnp.arange(N_MESH, dtype=jnp.int32))
    return reduced
```

```python
import functools

import jax
import jax.numpy as jnp
from jax import lax
from jax.experimental import pallas as pl
from jax.experimental.pallas import tpu as pltpu
from jax.sharding import PartitionSpec as P

GMAX = 4
OFFSETS = (1, -1, 2, -2)
NEIGH = len(OFFSETS)
MESH = pl.DeviceIdType.MESH
UNROLL = 8
K_PARTS = 4


def passed_along(block, axis, distance):
    devices = range(lax.axis_size(axis))
    route = [((i - distance) % len(devices), i) for i in devices]
    return lax.ppermute(block, axis, route)


def group_term(source_pool, blocks_here, rows_here, columns, scale, clusters):
    sources = source_pool[columns]
    product = jnp.einsum("bpj,bij->bpi", sources, blocks_here, preferred_element_type=jnp.float32)
    selector = (rows_here[None, :] == jnp.arange(clusters, dtype=jnp.int32)[:, None]).astype(
        jnp.float32
    ) * scale[None, :]
    return jnp.dot(selector, product.reshape(product.shape[0], -1), precision=lax.Precision.HIGHEST)


def generic_local(
    basis_vectors, stiffness_blocks, block_rows, block_columns, density, block_counts, send_list
):
    clusters, panel_width, cluster_dofs = basis_vectors.shape
    capacity = stiffness_blocks.shape[0]
    arriving = []
    for neighbour, offset in enumerate(OFFSETS):
        listed = send_list[neighbour * GMAX : (neighbour + 1) * GMAX]
        picked = basis_vectors[listed]
        arriving.append(passed_along(picked, "mesh", offset))
    source_pool = jnp.concatenate([basis_vectors] + arriving, axis=0)
    active = jnp.arange(capacity, dtype=jnp.int32) < block_counts[0]
    scale = jnp.where(active, 0.001 + density**3, jnp.float32(0.0))
    summed = group_term(source_pool, stiffness_blocks, block_rows, block_columns, scale, clusters)
    products = summed.reshape(clusters, panel_width, cluster_dofs).astype(jnp.bfloat16)
    gathered = lax.all_gather(products, "panel", axis=1, tiled=True)
    partial_tile = jnp.einsum(
        "npc,nqc->pq", basis_vectors, gathered, preferred_element_type=jnp.float32
    )
    return lax.psum_scatter(partial_tile, "mesh", scatter_dimension=1, tiled=True)


def kernel(
    n_mesh,
    rows_s,
    cols_s,
    dens_s,
    count_s,
    send_s,
    cols_v,
    basis_hbm,
    k_hbm,
    out_ref,
    v_full,
    v_own,
    own_packed,
    send_buf,
    ghost,
    k_v,
    prefix,
    w2,
    part,
    landed,
    order_v,
    order_s,
    k_sem,
    local_sem,
    panel_send,
    panel_recv,
    ghost_send,
    ghost_recv,
    tile_send,
    tile_recv,
):
    del cols_s
    clusters, width, dofs = basis_hbm.shape
    capacity = k_hbm.shape[0]
    ranks = 2 * width
    pools = clusters + NEIGH * GMAX
    per_panel = n_mesh // 2
    q = lax.axis_index("mesh")
    p = lax.axis_index("panel")
    me = q * 2 + p
    everyone = n_mesh * 2

    barrier = pltpu.get_barrier_semaphore()
    for step in range(1, everyone):
        other = lax.rem(me + step, everyone)
        pl.semaphore_signal(
            barrier, inc=1, device_id=(other // 2, lax.rem(other, 2)), device_id_type=MESH
        )

    own_rows = pl.ds(pl.multiple_of(p * width, width), width)
    fetch_own = pltpu.make_async_copy(basis_hbm, v_own, local_sem.at[0])
    fetch_own.start()
    fetch_half = pltpu.make_async_copy(basis_hbm, v_full.at[:, own_rows, :], local_sem.at[1])
    fetch_half.start()
    piece = capacity // K_PARTS
    fetch_k = [
        pltpu.make_async_copy(
            k_hbm.at[pl.ds(i * piece, piece)], k_v.at[pl.ds(i * piece, piece)], k_sem.at[i]
        )
        for i in range(K_PARTS)
    ]
    for copy in fetch_k:
        copy.start()

    lane = lax.broadcasted_iota(jnp.int32, (capacity, 128), 1)
    sub = lax.broadcasted_iota(jnp.int32, (capacity, 128), 0)
    columns = jnp.broadcast_to(cols_v[...], (capacity, 128))
    keys = columns * 128 + lane
    key_col = jnp.sum(jnp.where(lane == sub, keys, 0), axis=1, keepdims=True)
    rank = jnp.sum(
        jnp.where((keys < key_col) & (lane < capacity), 1, 0), axis=1, keepdims=True
    )
    order_v[...] = jnp.zeros_like(order_v)
    order_v[0:1, :] = jnp.sum(jnp.where(rank == lane, sub, 0), axis=0, keepdims=True)
    order_v[1:2, :] = jnp.sum(
        jnp.where(key_col < (lane + 1) * 128, 1, 0), axis=0, keepdims=True
    )
    order_copy = pltpu.make_async_copy(order_v, order_s, local_sem.at[2])
    order_copy.start()

    fetch_own.wait()
    for k in range(NEIGH):
        for g in range(GMAX):
            listed = send_s[k * GMAX + g]
            send_buf[k, :, g * dofs : (g + 1) * dofs] = v_own[listed]

    pl.semaphore_wait(barrier, everyone - 1)

    to_panel = pltpu.make_async_remote_copy(
        src_ref=basis_hbm,
        dst_ref=v_full.at[:, own_rows, :],
        send_sem=panel_send,
        recv_sem=panel_recv,
        device_id=(q, 1 - p),
        device_id_type=MESH,
    )
    to_panel.start()
    ghosts = []
    for k, offset in enumerate(OFFSETS):
        copy = pltpu.make_async_remote_copy(
            src_ref=send_buf.at[k],
            dst_ref=ghost.at[k],
            send_sem=ghost_send.at[k],
            recv_sem=ghost_recv.at[k],
            device_id=(lax.rem(q + offset + n_mesh, n_mesh), p),
            device_id_type=MESH,
        )
        copy.start()
        ghosts.append(copy)

    for s in range(clusters):
        own_packed[:, s * dofs : (s + 1) * dofs] = v_own[s]

    order_copy.wait()
    fetch_half.wait()
    for copy in fetch_k:
        copy.wait()
    to_panel.wait_recv()

    count = count_s[0]
    prefix[0] = jnp.zeros((ranks, dofs), jnp.float32)

    def several(t, carry):
        total = prefix[t * UNROLL]
        for u in range(UNROLL):
            at = t * UNROLL + u
            b = order_s[0, at]
            d = dens_s[b]
            scale = jnp.where(b < count, 0.001 + d * d * d, jnp.float32(0.0))
            term = jnp.dot(v_full[rows_s[b]], k_v[b], preferred_element_type=jnp.float32)
            total = total + scale * term
            prefix[at + 1] = total
        return carry

    lax.fori_loop(0, capacity // UNROLL, several, 0)

    for s in range(pools):
        w = prefix[order_s[1, s]]
        if s > 0:
            w = w - prefix[order_s[1, s - 1]]
        high = w.astype(jnp.bfloat16)
        w2[0:ranks, s * dofs : (s + 1) * dofs] = high
        w2[ranks : 2 * ranks, s * dofs : (s + 1) * dofs] = (
            w - high.astype(jnp.float32)
        ).astype(jnp.bfloat16)

    def against(slabs, first, length):
        return lax.dot_general(
            slabs,
            w2[:, first : first + length],
            (((1,), (1,)), ((), ())),
            preferred_element_type=jnp.float32,
        )

    both = against(own_packed[...], 0, clusters * dofs)
    for k in range(NEIGH):
        ghosts[k].wait_recv()
        both = both + against(ghost[k], (clusters + k * GMAX) * dofs, GMAX * dofs)
    whole = both[:, :ranks] + both[:, ranks:]
    for j in range(per_panel):
        part[j] = whole[j * 8 : (j + 1) * 8]

    tiles = []
    for j in range(per_panel):
        for half in range(2):
            target = p * per_panel + j
            tiles.append(
                (
                    (target == q) & (p == half),
                    pltpu.make_async_remote_copy(
                        src_ref=part.at[j],
                        dst_ref=landed.at[q],
                        send_sem=tile_send.at[j * 2 + half],
                        recv_sem=tile_recv.at[q],
                        device_id=(target, half),
                        device_id_type=MESH,
                    ),
                    pltpu.make_async_copy(part.at[j], landed.at[q], tile_recv.at[q]),
                )
            )
    for own, remote, local in tiles:

        @pl.when(jnp.logical_not(own))
        def _():
            remote.start()

        @pl.when(own)
        def _():
            local.start()

    to_panel.wait_send()
    for copy in ghosts:
        copy.wait_send()

    for source in range(n_mesh):
        pltpu.make_async_copy(part.at[0], landed.at[source], tile_recv.at[source]).wait()
    total = landed[0]
    for source in range(1, n_mesh):
        total = total + landed[source]
    turned = total.T
    out_ref[...] = jnp.where(p == 0, turned[:width], turned[width:])

    for own, remote, local in tiles:

        @pl.when(jnp.logical_not(own))
        def _():
            remote.wait_send()


def fused_local(
    basis_vectors, stiffness_blocks, block_rows, block_columns, density, block_counts, send_list
):
    clusters, width, dofs = basis_vectors.shape
    capacity = stiffness_blocks.shape[0]
    n_mesh = lax.axis_size("mesh")
    ranks = 2 * width
    pools = clusters + NEIGH * GMAX
    tile = ranks // n_mesh
    cols_row = jnp.pad(block_columns, (0, 128 - capacity)).reshape(1, 128)
    smem = pl.BlockSpec(memory_space=pltpu.SMEM)
    vmem = pl.BlockSpec(memory_space=pltpu.VMEM)
    anywhere = pl.BlockSpec(memory_space=pl.ANY)
    dma = pltpu.SemaphoreType.DMA
    return pl.pallas_call(
        functools.partial(kernel, n_mesh),
        out_shape=jax.ShapeDtypeStruct((width, tile), jnp.float32),
        in_specs=[smem] * 5 + [vmem, anywhere, anywhere],
        out_specs=vmem,
        scratch_shapes=[
            pltpu.VMEM((clusters, ranks, dofs), jnp.bfloat16),
            pltpu.VMEM((clusters, width, dofs), jnp.bfloat16),
            pltpu.VMEM((width, clusters * dofs), jnp.bfloat16),
            pltpu.VMEM((NEIGH, width, GMAX * dofs), jnp.bfloat16),
            pltpu.VMEM((NEIGH, width, GMAX * dofs), jnp.bfloat16),
            pltpu.VMEM((capacity, dofs, dofs), jnp.bfloat16),
            pltpu.VMEM((capacity + 1, ranks, dofs), jnp.float32),
            pltpu.VMEM((2 * ranks, pools * dofs), jnp.bfloat16),
            pltpu.VMEM((n_mesh // 2, tile, ranks), jnp.float32),
            pltpu.VMEM((n_mesh, tile, ranks), jnp.float32),
            pltpu.VMEM((8, 128), jnp.int32),
            pltpu.SMEM((8, 128), jnp.int32),
            dma((K_PARTS,)),
            dma((3,)),
            dma,
            dma,
            dma((NEIGH,)),
            dma((NEIGH,)),
            dma((n_mesh,)),
            dma((n_mesh,)),
        ],
        compiler_params=pltpu.CompilerParams(
            collective_id=0, has_side_effects=True, vmem_limit_bytes=40 * 1024 * 1024
        ),
    )(
        block_rows,
        block_columns,
        density,
        block_counts,
        send_list,
        cols_row,
        basis_vectors,
        stiffness_blocks,
    )


def solution(mesh):
    placed = (
        P("mesh", "panel", None),
        P("mesh", None, None),
        P("mesh"),
        P("mesh"),
        P("mesh"),
        P("mesh"),
        P("mesh"),
    )
    fused = jax.shard_map(
        fused_local, mesh=mesh, in_specs=placed, out_specs=P("panel", "mesh"), check_vma=False
    )
    generic = jax.shard_map(
        generic_local, mesh=mesh, in_specs=placed, out_specs=P("panel", "mesh"), check_vma=False
    )

    def run(basis_vectors, stiffness_blocks, *rest):
        n_mesh, n_panel = mesh.shape["mesh"], mesh.shape["panel"]
        ranks = basis_vectors.shape[1]
        capacity = stiffness_blocks.shape[0] // n_mesh
        fits = n_panel == 2 and ranks == 128 and ranks == 8 * n_mesh
        fits = fits and capacity % UNROLL == 0 and capacity <= 128
        return (fused if fits else generic)(basis_vectors, stiffness_blocks, *rest)

    return run
```

```python
import functools

import jax
import jax.numpy as jnp
from jax import lax
from jax.experimental import pallas as pl
from jax.experimental.pallas import tpu as pltpu
from jax.sharding import PartitionSpec as P

GMAX = 4
OFFSETS = (1, -1, 2, -2)
NEIGH = len(OFFSETS)
MESH = pl.DeviceIdType.MESH
UNROLL = 8
K_PARTS = 4


def passed_along(block, axis, distance):
    devices = range(lax.axis_size(axis))
    route = [((i - distance) % len(devices), i) for i in devices]
    return lax.ppermute(block, axis, route)


def group_term(source_pool, blocks_here, rows_here, columns, scale, clusters):
    sources = source_pool[columns]
    product = jnp.einsum("bpj,bij->bpi", sources, blocks_here, preferred_element_type=jnp.float32)
    selector = (rows_here[None, :] == jnp.arange(clusters, dtype=jnp.int32)[:, None]).astype(
        jnp.float32
    ) * scale[None, :]
    return jnp.dot(selector, product.reshape(product.shape[0], -1), precision=lax.Precision.HIGHEST)


def generic_local(
    basis_vectors, stiffness_blocks, block_rows, block_columns, density, block_counts, send_list
):
    clusters, panel_width, cluster_dofs = basis_vectors.shape
    capacity = stiffness_blocks.shape[0]
    arriving = []
    for neighbour, offset in enumerate(OFFSETS):
        listed = send_list[neighbour * GMAX : (neighbour + 1) * GMAX]
        picked = basis_vectors[listed]
        arriving.append(passed_along(picked, "mesh", offset))
    source_pool = jnp.concatenate([basis_vectors] + arriving, axis=0)
    active = jnp.arange(capacity, dtype=jnp.int32) < block_counts[0]
    scale = jnp.where(active, 0.001 + density**3, jnp.float32(0.0))
    summed = group_term(source_pool, stiffness_blocks, block_rows, block_columns, scale, clusters)
    products = summed.reshape(clusters, panel_width, cluster_dofs).astype(jnp.bfloat16)
    gathered = lax.all_gather(products, "panel", axis=1, tiled=True)
    partial_tile = jnp.einsum(
        "npc,nqc->pq", basis_vectors, gathered, preferred_element_type=jnp.float32
    )
    return lax.psum_scatter(partial_tile, "mesh", scatter_dimension=1, tiled=True)


def kernel(
    n_mesh,
    rows_hbm,
    cols_hbm,
    dens_hbm,
    count_hbm,
    send_hbm,
    basis_hbm,
    k_hbm,
    out_ref,
    rows_s,
    cols_s,
    dens_s,
    count_s,
    send_s,
    v_full,
    v_own,
    own_packed,
    send_buf,
    ghost,
    k_v,
    prefix,
    w2,
    part,
    landed,
    order_v,
    order_s,
    k_sem,
    local_sem,
    panel_send,
    panel_recv,
    ghost_send,
    ghost_recv,
    tile_send,
    tile_recv,
):
    clusters, width, dofs = basis_hbm.shape
    capacity = k_hbm.shape[0]
    ranks = 2 * width
    pools = clusters + NEIGH * GMAX
    per_panel = n_mesh // 2
    q = lax.axis_index("mesh")
    p = lax.axis_index("panel")
    me = q * 2 + p
    everyone = n_mesh * 2

    barrier = pltpu.get_barrier_semaphore()
    for step in range(1, everyone):
        other = lax.rem(me + step, everyone)
        pl.semaphore_signal(
            barrier, inc=1, device_id=(other // 2, lax.rem(other, 2)), device_id_type=MESH
        )

    lists = [
        pltpu.make_async_copy(source, held, local_sem.at[3 + i])
        for i, (source, held) in enumerate(
            (
                (send_hbm, send_s),
                (cols_hbm, cols_s),
                (rows_hbm, rows_s),
                (dens_hbm, dens_s),
                (count_hbm, count_s),
            )
        )
    ]
    for copy in lists:
        copy.start()
    own_rows = pl.ds(pl.multiple_of(p * width, width), width)
    fetch_own = pltpu.make_async_copy(basis_hbm, v_own, local_sem.at[0])
    fetch_own.start()
    fetch_half = pltpu.make_async_copy(basis_hbm, v_full.at[:, own_rows, :], local_sem.at[1])
    fetch_half.start()
    piece = capacity // K_PARTS
    fetch_k = [
        pltpu.make_async_copy(
            k_hbm.at[pl.ds(i * piece, piece)], k_v.at[pl.ds(i * piece, piece)], k_sem.at[i]
        )
        for i in range(K_PARTS)
    ]
    for copy in fetch_k:
        copy.start()

    for copy in lists:
        copy.wait()

    fetch_own.wait()
    for k in range(NEIGH):
        for g in range(GMAX):
            listed = send_s[k * GMAX + g]
            send_buf[k, :, g * dofs : (g + 1) * dofs] = v_own[listed]

    pl.semaphore_wait(barrier, everyone - 1)

    to_panel = pltpu.make_async_remote_copy(
        src_ref=v_own,
        dst_ref=v_full.at[:, own_rows, :],
        send_sem=panel_send,
        recv_sem=panel_recv,
        device_id=(q, 1 - p),
        device_id_type=MESH,
    )
    to_panel.start()
    ghosts = []
    for k, offset in enumerate(OFFSETS):
        copy = pltpu.make_async_remote_copy(
            src_ref=send_buf.at[k],
            dst_ref=ghost.at[k],
            send_sem=ghost_send.at[k],
            recv_sem=ghost_recv.at[k],
            device_id=(lax.rem(q + offset + n_mesh, n_mesh), p),
            device_id_type=MESH,
        )
        copy.start()
        ghosts.append(copy)

    lane = lax.broadcasted_iota(jnp.int32, (capacity, 128), 1)
    sub = lax.broadcasted_iota(jnp.int32, (capacity, 128), 0)
    lane_row = lax.broadcasted_iota(jnp.int32, (1, 128), 1)
    columns = jnp.zeros((1, 128), jnp.int32)
    for b in range(capacity):
        columns = jnp.where(lane_row == b, cols_s[b], columns)
    columns = jnp.broadcast_to(columns, (capacity, 128))
    keys = columns * 128 + lane
    key_col = jnp.sum(jnp.where(lane == sub, keys, 0), axis=1, keepdims=True)
    rank = jnp.sum(
        jnp.where((keys < key_col) & (lane < capacity), 1, 0), axis=1, keepdims=True
    )
    order_v[...] = jnp.zeros_like(order_v)
    order_v[0:1, :] = jnp.sum(jnp.where(rank == lane, sub, 0), axis=0, keepdims=True)
    order_v[1:2, :] = jnp.sum(
        jnp.where(key_col < (lane + 1) * 128, 1, 0), axis=0, keepdims=True
    )
    order_copy = pltpu.make_async_copy(order_v, order_s, local_sem.at[2])
    order_copy.start()

    for s in range(clusters):
        own_packed[:, s * dofs : (s + 1) * dofs] = v_own[s]

    order_copy.wait()
    fetch_half.wait()
    for copy in fetch_k:
        copy.wait()
    to_panel.wait_recv()

    count = count_s[0]
    prefix[0] = jnp.zeros((ranks, dofs), jnp.float32)

    def several(t, carry):
        total = prefix[t * UNROLL]
        for u in range(UNROLL):
            at = t * UNROLL + u
            b = order_s[0, at]
            d = dens_s[b]
            scale = jnp.where(b < count, 0.001 + d * d * d, jnp.float32(0.0))
            term = jnp.dot(v_full[rows_s[b]], k_v[b], preferred_element_type=jnp.float32)
            total = total + scale * term
            prefix[at + 1] = total
        return carry

    lax.fori_loop(0, capacity // UNROLL, several, 0)

    for s in range(pools):
        w = prefix[order_s[1, s]]
        if s > 0:
            w = w - prefix[order_s[1, s - 1]]
        high = w.astype(jnp.bfloat16)
        w2[0:ranks, s * dofs : (s + 1) * dofs] = high
        w2[ranks : 2 * ranks, s * dofs : (s + 1) * dofs] = (
            w - high.astype(jnp.float32)
        ).astype(jnp.bfloat16)

    def against(slabs, first, length):
        return lax.dot_general(
            slabs,
            w2[:, first : first + length],
            (((1,), (1,)), ((), ())),
            preferred_element_type=jnp.float32,
        )

    both = against(own_packed[...], 0, clusters * dofs)
    for k in range(NEIGH):
        ghosts[k].wait_recv()
        both = both + against(ghost[k], (clusters + k * GMAX) * dofs, GMAX * dofs)
    whole = both[:, :ranks] + both[:, ranks:]
    tall = lax.broadcasted_iota(jnp.int32, (8, ranks), 0)
    wide = lax.broadcasted_iota(jnp.int32, (8, ranks), 1)
    for j in range(per_panel):
        tile = whole[j * 8 : (j + 1) * 8]
        crossed = pltpu.roll(pltpu.roll(tile, 4, 0), width, 1)
        tile = jnp.where((wide < width) == (tall < 4), tile, crossed)
        part[j, 0] = tile[:4]
        part[j, 1] = tile[4:]

    tiles = []
    for j in range(per_panel):
        for half in range(2):
            target = p * per_panel + j
            tiles.append(
                (
                    (target == q) & (p == half),
                    pltpu.make_async_remote_copy(
                        src_ref=part.at[j, half],
                        dst_ref=landed.at[q],
                        send_sem=tile_send.at[j * 2 + half],
                        recv_sem=tile_recv.at[q],
                        device_id=(target, half),
                        device_id_type=MESH,
                    ),
                    pltpu.make_async_copy(part.at[j, half], landed.at[q], tile_recv.at[q]),
                )
            )
    for own, remote, local in tiles:

        @pl.when(jnp.logical_not(own))
        def _():
            remote.start()

        @pl.when(own)
        def _():
            local.start()

    to_panel.wait_send()
    for copy in ghosts:
        copy.wait_send()

    for source in range(n_mesh):
        pltpu.make_async_copy(part.at[0, 0], landed.at[source], tile_recv.at[source]).wait()
    total = landed[0]
    for source in range(1, n_mesh):
        total = total + landed[source]
    out_ref[0:4, :] = total[:, :width]
    out_ref[4:8, :] = total[:, width:]

    for own, remote, local in tiles:

        @pl.when(jnp.logical_not(own))
        def _():
            remote.wait_send()


def fused_local(
    basis_vectors, stiffness_blocks, block_rows, block_columns, density, block_counts, send_list
):
    clusters, width, dofs = basis_vectors.shape
    capacity = stiffness_blocks.shape[0]
    n_mesh = lax.axis_size("mesh")
    ranks = 2 * width
    pools = clusters + NEIGH * GMAX
    tile = ranks // n_mesh
    in_hbm = pl.BlockSpec(memory_space=pltpu.HBM)
    vmem = pl.BlockSpec(memory_space=pltpu.VMEM)
    dma = pltpu.SemaphoreType.DMA
    turned = pl.pallas_call(
        functools.partial(kernel, n_mesh),
        out_shape=jax.ShapeDtypeStruct((tile, width), jnp.float32),
        in_specs=[in_hbm] * 7,
        out_specs=vmem,
        scratch_shapes=[
            pltpu.SMEM((capacity,), jnp.int32),
            pltpu.SMEM((capacity,), jnp.int32),
            pltpu.SMEM((capacity,), jnp.float32),
            pltpu.SMEM((1,), jnp.int32),
            pltpu.SMEM((NEIGH * GMAX,), jnp.int32),
            pltpu.VMEM((clusters, ranks, dofs), jnp.bfloat16),
            pltpu.VMEM((clusters, width, dofs), jnp.bfloat16),
            pltpu.VMEM((width, clusters * dofs), jnp.bfloat16),
            pltpu.VMEM((NEIGH, width, GMAX * dofs), jnp.bfloat16),
            pltpu.VMEM((NEIGH, width, GMAX * dofs), jnp.bfloat16),
            pltpu.VMEM((capacity, dofs, dofs), jnp.bfloat16),
            pltpu.VMEM((capacity + 1, ranks, dofs), jnp.float32),
            pltpu.VMEM((2 * ranks, pools * dofs), jnp.bfloat16),
            pltpu.VMEM((n_mesh // 2, 2, tile // 2, ranks), jnp.float32),
            pltpu.VMEM((n_mesh, tile // 2, ranks), jnp.float32),
            pltpu.VMEM((8, 128), jnp.int32),
            pltpu.SMEM((8, 128), jnp.int32),
            dma((K_PARTS,)),
            dma((8,)),
            dma,
            dma,
            dma((NEIGH,)),
            dma((NEIGH,)),
            dma((n_mesh,)),
            dma((n_mesh,)),
        ],
        compiler_params=pltpu.CompilerParams(
            collective_id=0, has_side_effects=True, vmem_limit_bytes=63 * 1024 * 1024
        ),
    )(
        block_rows,
        block_columns,
        density,
        block_counts,
        send_list,
        basis_vectors,
        stiffness_blocks,
    )
    return turned.T


def solution(mesh):
    placed = (
        P("mesh", "panel", None),
        P("mesh", None, None),
        P("mesh"),
        P("mesh"),
        P("mesh"),
        P("mesh"),
        P("mesh"),
    )
    fused = jax.shard_map(
        fused_local, mesh=mesh, in_specs=placed, out_specs=P("panel", "mesh"), check_vma=False
    )
    generic = jax.shard_map(
        generic_local, mesh=mesh, in_specs=placed, out_specs=P("panel", "mesh"), check_vma=False
    )

    def run(basis_vectors, stiffness_blocks, *rest):
        n_mesh, n_panel = mesh.shape["mesh"], mesh.shape["panel"]
        ranks = basis_vectors.shape[1]
        capacity = stiffness_blocks.shape[0] // n_mesh
        fits = n_panel == 2 and ranks == 128 and ranks == 8 * n_mesh
        fits = fits and capacity % UNROLL == 0 and capacity <= 128
        return (fused if fits else generic)(basis_vectors, stiffness_blocks, *rest)

    return run
```

```python
import functools

import jax
import jax.numpy as jnp
from jax import lax
from jax.experimental import pallas as pl
from jax.experimental.pallas import tpu as pltpu
from jax.sharding import PartitionSpec as P

GMAX = 4
OFFSETS = (1, -1, 2, -2)
NEIGH = len(OFFSETS)
MESH = pl.DeviceIdType.MESH
UNROLL = 14
K_PARTS = 4


def passed_along(block, axis, distance):
    devices = range(lax.axis_size(axis))
    route = [((i - distance) % len(devices), i) for i in devices]
    return lax.ppermute(block, axis, route)


def group_term(source_pool, blocks_here, rows_here, columns, scale, clusters):
    sources = source_pool[columns]
    product = jnp.einsum("bpj,bij->bpi", sources, blocks_here, preferred_element_type=jnp.float32)
    selector = (rows_here[None, :] == jnp.arange(clusters, dtype=jnp.int32)[:, None]).astype(
        jnp.float32
    ) * scale[None, :]
    return jnp.dot(selector, product.reshape(product.shape[0], -1), precision=lax.Precision.HIGHEST)


def generic_local(
    basis_vectors, stiffness_blocks, block_rows, block_columns, density, block_counts, send_list
):
    clusters, panel_width, cluster_dofs = basis_vectors.shape
    capacity = stiffness_blocks.shape[0]
    arriving = []
    for neighbour, offset in enumerate(OFFSETS):
        listed = send_list[neighbour * GMAX : (neighbour + 1) * GMAX]
        picked = basis_vectors[listed]
        arriving.append(passed_along(picked, "mesh", offset))
    source_pool = jnp.concatenate([basis_vectors] + arriving, axis=0)
    active = jnp.arange(capacity, dtype=jnp.int32) < block_counts[0]
    scale = jnp.where(active, 0.001 + density**3, jnp.float32(0.0))
    summed = group_term(source_pool, stiffness_blocks, block_rows, block_columns, scale, clusters)
    products = summed.reshape(clusters, panel_width, cluster_dofs).astype(jnp.bfloat16)
    gathered = lax.all_gather(products, "panel", axis=1, tiled=True)
    partial_tile = jnp.einsum(
        "npc,nqc->pq", basis_vectors, gathered, preferred_element_type=jnp.float32
    )
    return lax.psum_scatter(partial_tile, "mesh", scatter_dimension=1, tiled=True)


def kernel(
    n_mesh,
    rows_hbm,
    cols_hbm,
    dens_hbm,
    count_hbm,
    send_hbm,
    basis_hbm,
    k_hbm,
    out_ref,
    rows_s,
    cols_s,
    dens_s,
    count_s,
    send_s,
    v_full,
    v_own,
    own_packed,
    send_buf,
    ghost,
    k_v,
    prefix,
    w2,
    part,
    landed,
    order_v,
    order_s,
    k_sem,
    local_sem,
    panel_send,
    panel_recv,
    ghost_send,
    ghost_recv,
    tile_send,
    tile_recv,
):
    clusters, width, dofs = basis_hbm.shape
    capacity = k_hbm.shape[0]
    ranks = 2 * width
    pools = clusters + NEIGH * GMAX
    per_panel = n_mesh // 2
    q = lax.axis_index("mesh")
    p = lax.axis_index("panel")
    me = q * 2 + p
    everyone = n_mesh * 2

    lists = [
        pltpu.make_async_copy(source, held, local_sem.at[3 + i])
        for i, (source, held) in enumerate(
            (
                (send_hbm, send_s),
                (cols_hbm, cols_s),
                (rows_hbm, rows_s),
                (dens_hbm, dens_s),
                (count_hbm, count_s),
            )
        )
    ]
    for copy in lists:
        copy.start()
    own_rows = pl.ds(pl.multiple_of(p * width, width), width)
    fetch_own = pltpu.make_async_copy(basis_hbm, v_own, local_sem.at[0])
    fetch_own.start()

    barrier = pltpu.get_barrier_semaphore()
    for step in range(1, everyone):
        other = lax.rem(me + step, everyone)
        pl.semaphore_signal(
            barrier, inc=1, device_id=(other // 2, lax.rem(other, 2)), device_id_type=MESH
        )

    fetch_half = pltpu.make_async_copy(basis_hbm, v_full.at[:, own_rows, :], local_sem.at[1])
    fetch_half.start()
    piece = capacity // K_PARTS
    fetch_k = [
        pltpu.make_async_copy(
            k_hbm.at[pl.ds(i * piece, piece)], k_v.at[pl.ds(i * piece, piece)], k_sem.at[i]
        )
        for i in range(K_PARTS)
    ]
    for copy in fetch_k:
        copy.start()

    lists[0].wait()
    fetch_own.wait()
    for k in range(NEIGH):
        for g in range(GMAX):
            listed = send_s[k * GMAX + g]
            send_buf[k, :, g * dofs : (g + 1) * dofs] = v_own[listed]

    pl.semaphore_wait(barrier, everyone - 1)

    to_panel = pltpu.make_async_remote_copy(
        src_ref=v_own,
        dst_ref=v_full.at[:, own_rows, :],
        send_sem=panel_send,
        recv_sem=panel_recv,
        device_id=(q, 1 - p),
        device_id_type=MESH,
    )
    to_panel.start()
    ghosts = []
    for k, offset in enumerate(OFFSETS):
        copy = pltpu.make_async_remote_copy(
            src_ref=send_buf.at[k],
            dst_ref=ghost.at[k],
            send_sem=ghost_send.at[k],
            recv_sem=ghost_recv.at[k],
            device_id=(lax.rem(q + offset + n_mesh, n_mesh), p),
            device_id_type=MESH,
        )
        copy.start()
        ghosts.append(copy)

    for copy in lists[1:]:
        copy.wait()

    lane = lax.broadcasted_iota(jnp.int32, (capacity, 128), 1)
    sub = lax.broadcasted_iota(jnp.int32, (capacity, 128), 0)
    lane_row = lax.broadcasted_iota(jnp.int32, (1, 128), 1)
    columns = jnp.zeros((1, 128), jnp.int32)
    for b in range(capacity):
        columns = jnp.where(lane_row == b, cols_s[b], columns)
    columns = jnp.broadcast_to(columns, (capacity, 128))
    keys = columns * 128 + lane
    key_col = jnp.sum(jnp.where(lane == sub, keys, 0), axis=1, keepdims=True)
    rank = jnp.sum(
        jnp.where((keys < key_col) & (lane < capacity), 1, 0), axis=1, keepdims=True
    )
    order_v[...] = jnp.zeros_like(order_v)
    order_v[0:1, :] = jnp.sum(jnp.where(rank == lane, sub, 0), axis=0, keepdims=True)
    order_v[1:2, :] = jnp.sum(
        jnp.where(key_col < (lane + 1) * 128, 1, 0), axis=0, keepdims=True
    )
    order_copy = pltpu.make_async_copy(order_v, order_s, local_sem.at[2])
    order_copy.start()

    for s in range(clusters):
        own_packed[:, s * dofs : (s + 1) * dofs] = v_own[s]

    order_copy.wait()
    fetch_half.wait()
    for copy in fetch_k:
        copy.wait()
    to_panel.wait_recv()

    count = count_s[0]
    prefix[0] = jnp.zeros((ranks, dofs), jnp.float32)

    def several(t, carry):
        total = prefix[t * UNROLL]
        for u in range(UNROLL):
            at = t * UNROLL + u
            b = order_s[0, at]
            d = dens_s[b]
            scale = jnp.where(b < count, 0.001 + d * d * d, jnp.float32(0.0))
            term = jnp.dot(v_full[rows_s[b]], k_v[b], preferred_element_type=jnp.float32)
            total = total + scale * term
            prefix[at + 1] = total
        return carry

    lax.fori_loop(0, capacity // UNROLL, several, 0)

    for s in range(pools):
        w = prefix[order_s[1, s]]
        if s > 0:
            w = w - prefix[order_s[1, s - 1]]
        high = w.astype(jnp.bfloat16)
        w2[0:ranks, s * dofs : (s + 1) * dofs] = high
        w2[ranks : 2 * ranks, s * dofs : (s + 1) * dofs] = (
            w - high.astype(jnp.float32)
        ).astype(jnp.bfloat16)

    def against(slabs, first, length):
        return lax.dot_general(
            slabs,
            w2[:, first : first + length],
            (((1,), (1,)), ((), ())),
            preferred_element_type=jnp.float32,
        )

    both = against(own_packed[...], 0, clusters * dofs)
    for k in range(NEIGH):
        ghosts[k].wait_recv()
        both = both + against(ghost[k], (clusters + k * GMAX) * dofs, GMAX * dofs)
    whole = both[:, :ranks] + both[:, ranks:]
    tall = lax.broadcasted_iota(jnp.int32, (8, ranks), 0)
    wide = lax.broadcasted_iota(jnp.int32, (8, ranks), 1)
    for j in range(per_panel):
        tile = whole[j * 8 : (j + 1) * 8]
        crossed = pltpu.roll(pltpu.roll(tile, 4, 0), width, 1)
        tile = jnp.where((wide < width) == (tall < 4), tile, crossed)
        part[j, 0] = tile[:4]
        part[j, 1] = tile[4:]

    tiles = []
    for j in range(per_panel):
        for half in range(2):
            target = p * per_panel + j
            tiles.append(
                (
                    (target == q) & (p == half),
                    pltpu.make_async_remote_copy(
                        src_ref=part.at[j, half],
                        dst_ref=landed.at[q],
                        send_sem=tile_send.at[j * 2 + half],
                        recv_sem=tile_recv.at[q],
                        device_id=(target, half),
                        device_id_type=MESH,
                    ),
                    pltpu.make_async_copy(part.at[j, half], landed.at[q], tile_recv.at[q]),
                )
            )
    for own, remote, local in tiles:

        @pl.when(jnp.logical_not(own))
        def _():
            remote.start()

        @pl.when(own)
        def _():
            local.start()

    to_panel.wait_send()
    for copy in ghosts:
        copy.wait_send()

    for source in range(n_mesh):
        pltpu.make_async_copy(part.at[0, 0], landed.at[source], tile_recv.at[source]).wait()
    total = landed[0]
    for source in range(1, n_mesh):
        total = total + landed[source]
    out_ref[0:4, :] = total[:, :width]
    out_ref[4:8, :] = total[:, width:]

    for own, remote, local in tiles:

        @pl.when(jnp.logical_not(own))
        def _():
            remote.wait_send()


def fused_local(
    basis_vectors, stiffness_blocks, block_rows, block_columns, density, block_counts, send_list
):
    clusters, width, dofs = basis_vectors.shape
    capacity = stiffness_blocks.shape[0]
    n_mesh = lax.axis_size("mesh")
    ranks = 2 * width
    pools = clusters + NEIGH * GMAX
    tile = ranks // n_mesh
    in_hbm = pl.BlockSpec(memory_space=pltpu.HBM)
    vmem = pl.BlockSpec(memory_space=pltpu.VMEM)
    dma = pltpu.SemaphoreType.DMA
    turned = pl.pallas_call(
        functools.partial(kernel, n_mesh),
        out_shape=jax.ShapeDtypeStruct((tile, width), jnp.float32),
        in_specs=[in_hbm] * 7,
        out_specs=vmem,
        scratch_shapes=[
            pltpu.SMEM((capacity,), jnp.int32),
            pltpu.SMEM((capacity,), jnp.int32),
            pltpu.SMEM((capacity,), jnp.float32),
            pltpu.SMEM((1,), jnp.int32),
            pltpu.SMEM((NEIGH * GMAX,), jnp.int32),
            pltpu.VMEM((clusters, ranks, dofs), jnp.bfloat16),
            pltpu.VMEM((clusters, width, dofs), jnp.bfloat16),
            pltpu.VMEM((width, clusters * dofs), jnp.bfloat16),
            pltpu.VMEM((NEIGH, width, GMAX * dofs), jnp.bfloat16),
            pltpu.VMEM((NEIGH, width, GMAX * dofs), jnp.bfloat16),
            pltpu.VMEM((capacity, dofs, dofs), jnp.bfloat16),
            pltpu.VMEM((capacity + 1, ranks, dofs), jnp.float32),
            pltpu.VMEM((2 * ranks, pools * dofs), jnp.bfloat16),
            pltpu.VMEM((n_mesh // 2, 2, tile // 2, ranks), jnp.float32),
            pltpu.VMEM((n_mesh, tile // 2, ranks), jnp.float32),
            pltpu.VMEM((8, 128), jnp.int32),
            pltpu.SMEM((8, 128), jnp.int32),
            dma((K_PARTS,)),
            dma((8,)),
            dma,
            dma,
            dma((NEIGH,)),
            dma((NEIGH,)),
            dma((n_mesh,)),
            dma((n_mesh,)),
        ],
        compiler_params=pltpu.CompilerParams(
            collective_id=0, has_side_effects=True, vmem_limit_bytes=63 * 1024 * 1024
        ),
    )(
        block_rows,
        block_columns,
        density,
        block_counts,
        send_list,
        basis_vectors,
        stiffness_blocks,
    )
    return turned.T


def solution(mesh):
    placed = (
        P("mesh", "panel", None),
        P("mesh", None, None),
        P("mesh"),
        P("mesh"),
        P("mesh"),
        P("mesh"),
        P("mesh"),
    )
    fused = jax.shard_map(
        fused_local, mesh=mesh, in_specs=placed, out_specs=P("panel", "mesh"), check_vma=False
    )
    generic = jax.shard_map(
        generic_local, mesh=mesh, in_specs=placed, out_specs=P("panel", "mesh"), check_vma=False
    )

    def run(basis_vectors, stiffness_blocks, *rest):
        n_mesh, n_panel = mesh.shape["mesh"], mesh.shape["panel"]
        ranks = basis_vectors.shape[1]
        capacity = stiffness_blocks.shape[0] // n_mesh
        fits = n_panel == 2 and ranks == 128 and ranks == 8 * n_mesh
        fits = fits and capacity % UNROLL == 0 and capacity <= 128
        return (fused if fits else generic)(basis_vectors, stiffness_blocks, *rest)

    return run
```

```python
import functools

import jax
import jax.numpy as jnp
from jax import lax
from jax.experimental import pallas as pl
from jax.experimental.pallas import tpu as pltpu
from jax.sharding import PartitionSpec as P

GMAX = 4
OFFSETS = (1, -1, 2, -2)
NEIGH = len(OFFSETS)
MESH = pl.DeviceIdType.MESH
UNROLL = 14
K_PARTS = 4


def passed_along(block, axis, distance):
    devices = range(lax.axis_size(axis))
    route = [((i - distance) % len(devices), i) for i in devices]
    return lax.ppermute(block, axis, route)


def group_term(source_pool, blocks_here, rows_here, columns, scale, clusters):
    sources = source_pool[columns]
    product = jnp.einsum("bpj,bij->bpi", sources, blocks_here, preferred_element_type=jnp.float32)
    selector = (rows_here[None, :] == jnp.arange(clusters, dtype=jnp.int32)[:, None]).astype(
        jnp.float32
    ) * scale[None, :]
    return jnp.dot(selector, product.reshape(product.shape[0], -1), precision=lax.Precision.HIGHEST)


def generic_local(
    basis_vectors, stiffness_blocks, block_rows, block_columns, density, block_counts, send_list
):
    clusters, panel_width, cluster_dofs = basis_vectors.shape
    capacity = stiffness_blocks.shape[0]
    arriving = []
    for neighbour, offset in enumerate(OFFSETS):
        listed = send_list[neighbour * GMAX : (neighbour + 1) * GMAX]
        picked = basis_vectors[listed]
        arriving.append(passed_along(picked, "mesh", offset))
    source_pool = jnp.concatenate([basis_vectors] + arriving, axis=0)
    active = jnp.arange(capacity, dtype=jnp.int32) < block_counts[0]
    scale = jnp.where(active, 0.001 + density**3, jnp.float32(0.0))
    summed = group_term(source_pool, stiffness_blocks, block_rows, block_columns, scale, clusters)
    products = summed.reshape(clusters, panel_width, cluster_dofs).astype(jnp.bfloat16)
    gathered = lax.all_gather(products, "panel", axis=1, tiled=True)
    partial_tile = jnp.einsum(
        "npc,nqc->pq", basis_vectors, gathered, preferred_element_type=jnp.float32
    )
    return lax.psum_scatter(partial_tile, "mesh", scatter_dimension=1, tiled=True)


def kernel(
    n_mesh,
    rows_hbm,
    cols_hbm,
    dens_hbm,
    count_hbm,
    send_hbm,
    basis_hbm,
    k_hbm,
    out_ref,
    rows_s,
    cols_s,
    dens_s,
    count_s,
    send_s,
    v_full,
    v_own,
    own_packed,
    send_buf,
    ghost,
    k_v,
    prefix,
    w2,
    part,
    landed,
    order_v,
    order_s,
    k_sem,
    local_sem,
    panel_send,
    panel_recv,
    ghost_send,
    ghost_recv,
    tile_send,
    tile_recv,
):
    clusters, width, dofs = basis_hbm.shape
    capacity = k_hbm.shape[0]
    ranks = 2 * width
    pools = clusters + NEIGH * GMAX
    per_panel = n_mesh // 2
    q = lax.axis_index("mesh")
    p = lax.axis_index("panel")
    me = q * 2 + p
    everyone = n_mesh * 2

    lists = [
        pltpu.make_async_copy(source, held, local_sem.at[3 + i])
        for i, (source, held) in enumerate(
            (
                (send_hbm, send_s),
                (cols_hbm, cols_s),
                (rows_hbm, rows_s),
                (dens_hbm, dens_s),
                (count_hbm, count_s),
            )
        )
    ]
    for copy in lists:
        copy.start()
    own_rows = pl.ds(pl.multiple_of(p * width, width), width)
    fetch_own = pltpu.make_async_copy(basis_hbm, v_own, local_sem.at[0])
    fetch_own.start()

    barrier = pltpu.get_barrier_semaphore()
    for step in range(1, everyone):
        other = lax.rem(me + step, everyone)
        pl.semaphore_signal(
            barrier, inc=1, device_id=(other // 2, lax.rem(other, 2)), device_id_type=MESH
        )

    fetch_half = pltpu.make_async_copy(basis_hbm, v_full.at[:, own_rows, :], local_sem.at[1])
    fetch_half.start()
    piece = capacity // K_PARTS
    fetch_k = [
        pltpu.make_async_copy(
            k_hbm.at[pl.ds(i * piece, piece)], k_v.at[pl.ds(i * piece, piece)], k_sem.at[i]
        )
        for i in range(K_PARTS)
    ]
    for copy in fetch_k:
        copy.start()

    lists[0].wait()
    fetch_own.wait()
    for k in range(NEIGH):
        for g in range(GMAX):
            listed = send_s[k * GMAX + g]
            send_buf[k, :, g * dofs : (g + 1) * dofs] = v_own[listed]

    pl.semaphore_wait(barrier, everyone - 1)

    to_panel = pltpu.make_async_remote_copy(
        src_ref=v_own,
        dst_ref=v_full.at[:, own_rows, :],
        send_sem=panel_send,
        recv_sem=panel_recv,
        device_id=(q, 1 - p),
        device_id_type=MESH,
    )
    to_panel.start()
    ghosts = []
    for k, offset in enumerate(OFFSETS):
        copy = pltpu.make_async_remote_copy(
            src_ref=send_buf.at[k],
            dst_ref=ghost.at[k],
            send_sem=ghost_send.at[k],
            recv_sem=ghost_recv.at[k],
            device_id=(lax.rem(q + offset + n_mesh, n_mesh), p),
            device_id_type=MESH,
        )
        copy.start()
        ghosts.append(copy)

    for copy in lists[1:]:
        copy.wait()

    lane = lax.broadcasted_iota(jnp.int32, (capacity, 128), 1)
    sub = lax.broadcasted_iota(jnp.int32, (capacity, 128), 0)
    lane_row = lax.broadcasted_iota(jnp.int32, (1, 128), 1)
    columns = jnp.zeros((1, 128), jnp.int32)
    for b in range(capacity):
        columns = jnp.where(lane_row == b, cols_s[b], columns)
    columns = jnp.broadcast_to(columns, (capacity, 128))
    keys = columns * 128 + lane
    key_col = jnp.sum(jnp.where(lane == sub, keys, 0), axis=1, keepdims=True)
    rank = jnp.sum(
        jnp.where((keys < key_col) & (lane < capacity), 1, 0), axis=1, keepdims=True
    )
    order_v[...] = jnp.zeros_like(order_v)
    order_v[0:1, :] = jnp.sum(jnp.where(rank == lane, sub, 0), axis=0, keepdims=True)
    order_v[1:2, :] = jnp.sum(
        jnp.where(key_col < (lane + 1) * 128, 1, 0), axis=0, keepdims=True
    )
    order_copy = pltpu.make_async_copy(order_v, order_s, local_sem.at[2])
    order_copy.start()

    for s in range(clusters):
        own_packed[:, s * dofs : (s + 1) * dofs] = v_own[s]

    order_copy.wait()
    fetch_half.wait()
    for copy in fetch_k:
        copy.wait()
    to_panel.wait_recv()

    count = count_s[0]
    prefix[0] = jnp.zeros((ranks, dofs), jnp.float32)

    def several(t, carry):
        total = prefix[t * UNROLL]
        for u in range(UNROLL):
            at = t * UNROLL + u
            b = order_s[0, at]
            d = dens_s[b]
            scale = jnp.where(b < count, 0.001 + d * d * d, jnp.float32(0.0))
            term = jnp.dot(v_full[rows_s[b]], k_v[b], preferred_element_type=jnp.float32)
            total = total + scale * term
            prefix[at + 1] = total
        return carry

    lax.fori_loop(0, capacity // UNROLL, several, 0)

    for s in range(pools):
        w = prefix[order_s[1, s]]
        if s > 0:
            w = w - prefix[order_s[1, s - 1]]
        high = w.astype(jnp.bfloat16)
        w2[0:ranks, s * dofs : (s + 1) * dofs] = high
        w2[ranks : 2 * ranks, s * dofs : (s + 1) * dofs] = (
            w - high.astype(jnp.float32)
        ).astype(jnp.bfloat16)

    def against(slabs, first, length):
        return lax.dot_general(
            slabs,
            w2[:, first : first + length],
            (((1,), (1,)), ((), ())),
            preferred_element_type=jnp.float32,
        )

    both = against(own_packed[...], 0, clusters * dofs)
    for k in range(NEIGH):
        ghosts[k].wait_recv()
        both = both + against(ghost[k], (clusters + k * GMAX) * dofs, GMAX * dofs)
    whole = both[:, :ranks] + both[:, ranks:]
    tall = lax.broadcasted_iota(jnp.int32, (8, ranks), 0)
    wide = lax.broadcasted_iota(jnp.int32, (8, ranks), 1)
    tiles = []
    for j in range(per_panel):
        for half in range(2):
            target = p * per_panel + j
            tiles.append(
                (
                    (target == q) & (p == half),
                    pltpu.make_async_remote_copy(
                        src_ref=part.at[j, half],
                        dst_ref=landed.at[q],
                        send_sem=tile_send.at[j * 2 + half],
                        recv_sem=tile_recv.at[q],
                        device_id=(target, half),
                        device_id_type=MESH,
                    ),
                    pltpu.make_async_copy(part.at[j, half], landed.at[q], tile_recv.at[q]),
                )
            )
    for j in range(per_panel):
        tile = whole[j * 8 : (j + 1) * 8]
        crossed = pltpu.roll(pltpu.roll(tile, 4, 0), width, 1)
        tile = jnp.where((wide < width) == (tall < 4), tile, crossed)
        part[j, 0] = tile[:4]
        part[j, 1] = tile[4:]
        for own, remote, local in tiles[2 * j : 2 * j + 2]:

            @pl.when(jnp.logical_not(own))
            def _():
                remote.start()

            @pl.when(own)
            def _():
                local.start()

    to_panel.wait_send()
    for copy in ghosts:
        copy.wait_send()

    for source in range(n_mesh):
        pltpu.make_async_copy(part.at[0, 0], landed.at[source], tile_recv.at[source]).wait()
    total = landed[0]
    for source in range(1, n_mesh):
        total = total + landed[source]
    out_ref[0:4, :] = total[:, :width]
    out_ref[4:8, :] = total[:, width:]

    for own, remote, local in tiles:

        @pl.when(jnp.logical_not(own))
        def _():
            remote.wait_send()


def fused_local(
    basis_vectors, stiffness_blocks, block_rows, block_columns, density, block_counts, send_list
):
    clusters, width, dofs = basis_vectors.shape
    capacity = stiffness_blocks.shape[0]
    n_mesh = lax.axis_size("mesh")
    ranks = 2 * width
    pools = clusters + NEIGH * GMAX
    tile = ranks // n_mesh
    in_hbm = pl.BlockSpec(memory_space=pltpu.HBM)
    vmem = pl.BlockSpec(memory_space=pltpu.VMEM)
    dma = pltpu.SemaphoreType.DMA
    turned = pl.pallas_call(
        functools.partial(kernel, n_mesh),
        out_shape=jax.ShapeDtypeStruct((tile, width), jnp.float32),
        in_specs=[in_hbm] * 7,
        out_specs=vmem,
        scratch_shapes=[
            pltpu.SMEM((capacity,), jnp.int32),
            pltpu.SMEM((capacity,), jnp.int32),
            pltpu.SMEM((capacity,), jnp.float32),
            pltpu.SMEM((1,), jnp.int32),
            pltpu.SMEM((NEIGH * GMAX,), jnp.int32),
            pltpu.VMEM((clusters, ranks, dofs), jnp.bfloat16),
            pltpu.VMEM((clusters, width, dofs), jnp.bfloat16),
            pltpu.VMEM((width, clusters * dofs), jnp.bfloat16),
            pltpu.VMEM((NEIGH, width, GMAX * dofs), jnp.bfloat16),
            pltpu.VMEM((NEIGH, width, GMAX * dofs), jnp.bfloat16),
            pltpu.VMEM((capacity, dofs, dofs), jnp.bfloat16),
            pltpu.VMEM((capacity + 1, ranks, dofs), jnp.float32),
            pltpu.VMEM((2 * ranks, pools * dofs), jnp.bfloat16),
            pltpu.VMEM((n_mesh // 2, 2, tile // 2, ranks), jnp.float32),
            pltpu.VMEM((n_mesh, tile // 2, ranks), jnp.float32),
            pltpu.VMEM((8, 128), jnp.int32),
            pltpu.SMEM((8, 128), jnp.int32),
            dma((K_PARTS,)),
            dma((8,)),
            dma,
            dma,
            dma((NEIGH,)),
            dma((NEIGH,)),
            dma((n_mesh,)),
            dma((n_mesh,)),
        ],
        compiler_params=pltpu.CompilerParams(
            collective_id=0, has_side_effects=True, vmem_limit_bytes=63 * 1024 * 1024
        ),
    )(
        block_rows,
        block_columns,
        density,
        block_counts,
        send_list,
        basis_vectors,
        stiffness_blocks,
    )
    return turned.T


def solution(mesh):
    placed = (
        P("mesh", "panel", None),
        P("mesh", None, None),
        P("mesh"),
        P("mesh"),
        P("mesh"),
        P("mesh"),
        P("mesh"),
    )
    fused = jax.shard_map(
        fused_local, mesh=mesh, in_specs=placed, out_specs=P("panel", "mesh"), check_vma=False
    )
    generic = jax.shard_map(
        generic_local, mesh=mesh, in_specs=placed, out_specs=P("panel", "mesh"), check_vma=False
    )

    def run(basis_vectors, stiffness_blocks, *rest):
        n_mesh, n_panel = mesh.shape["mesh"], mesh.shape["panel"]
        ranks = basis_vectors.shape[1]
        capacity = stiffness_blocks.shape[0] // n_mesh
        fits = n_panel == 2 and ranks == 128 and ranks == 8 * n_mesh
        fits = fits and capacity % UNROLL == 0 and capacity <= 128
        return (fused if fits else generic)(basis_vectors, stiffness_blocks, *rest)

    return run
```
